512 devices in a mesh: outer: 16 (over y_lo, z), inner: 32 (over x, y_hi, core).
Axes of the slice: x: 4, y: 8 (y_hi: 4, y_lo: 2; y = y_hi * 2 + y_lo), z: 8, core: 2. Of those that a mesh axis runs over, the one named last changes fastest.
Arguments:
- queries: bfloat16 [65536, 8192], P(('outer', 'inner')), may hold values from -8 to 8
- keys: bfloat16 [65536, 512], P(('outer', 'inner')), may hold values from -8 to 8
- values: bfloat16 [65536, 512], P(('outer', 'inner')), may hold values from -6 to 6
- doc_ids: int32 [65536], P(('outer', 'inner')), may hold values from 0 to 3, never falling along the last dimension, each value on 1 to 32768 neighbouring positions
Outputs:
- attended: bfloat16 [65536, 8192], P(('outer', 'inner'))
- log_norm: float32 [64, 65536], P(None, ('outer', 'inner'))
The draws below stay inside these ranges and needn't reach their ends.
Inputs may be any that keep to these rules, and one draw needn't show every extreme that they name: `doc_ids`: document numbers never fall along the sequence; each document is 1 to 32768 tokens.
All inputs are finite; a program needn't handle non-finite values.
Results may differ from the reference program's by a relative error of at most 0.006.
Values may be sent and summed in bfloat16 or wider, within the bound.
A program may use at most 128 MiB of HBM per device.

```python
import math
import jax
import jax.numpy as jnp
import numpy as np
from jax import lax

QUERY_HEADS = 64
KEY_VALUE_HEADS = 4
HEAD_WIDTH = 128
BLK = 128
DOCS = 4
SEQUENCE_TOKENS = 65536
DOC_MOST = 32768
N_OUTER = 16
N_INNER = 32


def draw_queries(key, part):
    key = jax.random.fold_in(key, 11)
    base_offset = jax.random.truncated_normal(key, -8.0, 8.0, (SEQUENCE_TOKENS, QUERY_HEADS * HEAD_WIDTH), jnp.float32)
    return base_offset.astype(jnp.bfloat16)


def draw_keys(key, part):
    key = jax.random.fold_in(key, 12)
    base_offset = jax.random.truncated_normal(key, -8.0, 8.0, (SEQUENCE_TOKENS, KEY_VALUE_HEADS * HEAD_WIDTH), jnp.float32)
    return base_offset.astype(jnp.bfloat16)


def levels(key, dims, split, least, top_value):
    def one(dim, parts):
        steps = jax.random.uniform(jax.random.fold_in(jax.random.fold_in(key, 6), dim), (parts,), jnp.float32, least / len(split), top_value / len(split))
        return jnp.repeat(jnp.exp(steps), dims[dim] // parts).reshape((-1,) + (1,) * (len(dims) - dim - 1))

    factor_of = one(*split[0])
    for cut in split[1:]:
        factor_of = factor_of * one(*cut)
    return factor_of


def profile(number_of, total, most, lean):
    loads = [(1 << 20) // math.isqrt(grade ** lean) + 1 for grade in range(2, number_of + 1)]
    rest, given = total - most - (number_of - 1), [1] * (number_of - 1)
    while rest > 0:
        candidates = [i for i in range(number_of - 1) if given[i] < most]
        whole, left = sum([loads[i] for i in candidates]), rest
        for i in candidates:
            more = min(most - given[i], max(1, left * loads[i] // whole), rest)
            given[i] = given[i] + more
            rest = rest - more
    return np.array([most] + given)


def uneven(stream_key, amount, total, bound, slope):
    if amount == 2:
        one = jax.random.randint(stream_key, (), max(1, total - bound), min(bound, total - 1) + 1)
        return jnp.stack([one, total - one])
    lengths = jnp.asarray(profile(amount, total, bound, slope), jnp.int32)
    pairs = (amount - 1) // 2
    donor, sink = lengths[1:1 + 2 * pairs:2], lengths[2:2 + 2 * pairs:2]
    margin = jnp.minimum(donor - 1, bound - sink)
    passed = jax.random.randint(jax.random.fold_in(stream_key, 1), (pairs,), 0, 1 << 20) % (margin + 1)
    lengths = lengths.at[1:1 + 2 * pairs:2].set(donor - passed).at[2:2 + 2 * pairs:2].set(sink + passed)
    return lengths[jax.random.permutation(jax.random.fold_in(stream_key, 2), amount)]


def centred(rng, dims, scale, bound, cuts=(), kind=jnp.bfloat16):
    array = scale * jax.random.normal(rng, dims, jnp.float32)
    if cuts:
        array = array * levels(rng, dims, cuts, -0.22, 0.18)
    return jnp.clip(array, -bound, bound).astype(kind)


def setup_inputs(seed: int = 0) -> dict:
    streams_of = jax.random.split(jax.random.key(seed), 5)
    return {
        "queries": draw_queries(jax.random.fold_in(streams_of[4], 71), 0),
        "keys": draw_keys(jax.random.fold_in(streams_of[4], 71), 0),
        "values": centred(streams_of[2], (SEQUENCE_TOKENS, KEY_VALUE_HEADS * HEAD_WIDTH), 1.0, 6.0, ((0, 512),)),
        "doc_ids": jnp.searchsorted(jnp.cumsum(uneven(streams_of[3], DOCS, SEQUENCE_TOKENS, DOC_MOST, 2)), jnp.arange(SEQUENCE_TOKENS), side="right").astype(jnp.int32),
    }


floor_score = -1e30


def block_terms(query_block, key_block, value_block, visible):
    rows = query_block.shape[0]
    key_heads = key_block.shape[1] // HEAD_WIDTH
    group = query_block.shape[1] // key_block.shape[1]
    query_wide = query_block.astype(jnp.float32).reshape(rows, key_heads, group, HEAD_WIDTH)
    key_wide = key_block.astype(jnp.float32).reshape(rows, key_heads, HEAD_WIDTH)
    value_wide = value_block.astype(jnp.float32).reshape(rows, key_heads, HEAD_WIDTH)
    scores = jnp.einsum("tkgd,jkd->kgtj", query_wide, key_wide) * (HEAD_WIDTH ** -0.5)
    masked = jnp.where(visible, scores, floor_score)
    peak = jnp.max(masked, axis=-1)
    weights = jnp.where(visible, jnp.exp(scores - peak[..., None]), 0.0).astype(jnp.bfloat16)
    weights_wide = weights.astype(jnp.float32)
    total = jnp.sum(weights_wide, axis=-1)
    weighted = jnp.einsum("kgtj,jkd->tkgd", weights_wide, value_wide)
    return peak, total, weighted


def reference(queries, keys, values, doc_ids):
    rows = BLK
    block_count = N_OUTER * N_INNER
    offsets = [0, 1, 2, N_INNER, 2 * N_INNER]
    local = jnp.arange(rows, dtype=jnp.int32)
    causal = local[:, None] >= local[None, :]

    def one_block(index):
        start = (index * rows).astype(jnp.int32)
        query_block = lax.dynamic_slice_in_dim(queries, start, rows, 0)
        query_docs = lax.dynamic_slice_in_dim(doc_ids, start, rows, 0)
        peaks, totals, sums = [], [], []
        for offset in offsets:
            source = (jnp.maximum(index - offset, 0) * rows).astype(jnp.int32)
            key_block = lax.dynamic_slice_in_dim(keys, source, rows, 0)
            value_block = lax.dynamic_slice_in_dim(values, source, rows, 0)
            key_docs = lax.dynamic_slice_in_dim(doc_ids, source, rows, 0)
            same = query_docs[:, None] == key_docs[None, :]
            if offset == 0:
                visible = same & causal
            else:
                visible = same & (index >= offset)
            peak_c, total_c, part_c = block_terms(query_block, key_block, value_block, visible)
            peaks.append(peak_c)
            totals.append(total_c)
            sums.append(part_c)
        peak_all = jnp.stack(peaks)
        peak = jnp.max(peak_all, axis=0)
        scales = jnp.exp(peak_all - peak[None])
        denominator = jnp.sum(scales * jnp.stack(totals), axis=0)
        numerator = jnp.sum(jnp.transpose(scales, (0, 3, 1, 2))[..., None] * jnp.stack(sums), axis=0)
        output = (numerator / jnp.transpose(denominator, (2, 0, 1))[..., None]).reshape(rows, -1).astype(jnp.bfloat16)
        log_total = (peak + jnp.log(denominator)).reshape(-1, rows)
        return output, log_total

    outputs, log_totals = lax.map(one_block, jnp.arange(block_count, dtype=jnp.int32))
    attended = outputs.reshape(SEQUENCE_TOKENS, QUERY_HEADS * HEAD_WIDTH)
    log_norm = jnp.transpose(log_totals, (1, 0, 2)).reshape(QUERY_HEADS, SEQUENCE_TOKENS)
    return attended, log_norm
```

```python
import functools
import math

import jax
import jax.numpy as jnp
from jax import lax
from jax.experimental import pallas as pl
from jax.experimental.pallas import tpu as pltpu
from jax.sharding import PartitionSpec as P

MESH = pl.DeviceIdType.MESH
WIDTH = 128
KV = 4
GROUP = 16
STACK = 4
STEPS = KV * GROUP // STACK
PER = GROUP // STACK
HIDE = -65536.0
SCALE = 1.0 / math.sqrt(WIDTH)
SCALE2 = SCALE * math.log2(math.e)
VMEM = 60 * 2**20
ABSENT = 4.0
ROWS = 2 * WIDTH + 16

OWN, NEAR, SECOND, FAR, DISTANT = range(5)


def nt(a, b):
    return lax.dot_general(a, b, (((1,), (1,)), ((), ())), preferred_element_type=jnp.float32)


def kernel(
    n_outer, n_inner, q_hbm, k_hbm, v_hbm, doc_hbm, o_hbm, log_ref,
    queries, result, got, seen_by, marks, peaks, totals, scores, weights,
    doc_ref, stage_sem, q_sem, o_sem, doc_sem, send_sem, recv_sem,
):
    outer, inner = lax.axis_index("outer"), lax.axis_index("inner")
    core = lax.rem(inner, 2)
    place = outer * n_inner + inner
    count = n_outer * n_inner

    def device(where):
        where = jnp.clip(where, 0, count - 1)
        return (where // n_inner, lax.rem(where, n_inner))

    has_far, gives_far = outer >= 1, outer < n_outer - 1
    has_distant = outer >= 2
    has_second, gives_second = place >= 2, place + 2 < count
    partner = (outer, inner + 1 - 2 * core)
    ahead = (jnp.minimum(outer + 1, n_outer - 1), inner)
    behind = (jnp.maximum(outer - 1, 0), inner)

    doc_copy = pltpu.make_async_copy(doc_hbm, doc_ref, doc_sem)
    doc_copy.start()
    staged = []
    for g in range(KV):
        for i, ref in enumerate((k_hbm, v_hbm)):
            copy = pltpu.make_async_copy(
                ref.at[:, pl.ds(g * WIDTH, WIDTH)],
                got.at[OWN, g, pl.ds(i * WIDTH, WIDTH)],
                stage_sem.at[g, i],
            )
            copy.start()
            staged.append(copy)
    fetch = []
    wide = GROUP * WIDTH
    for g in range(KV):
        copy = pltpu.make_async_copy(
            q_hbm.at[:, pl.ds(g * wide, wide)], queries.at[:, pl.ds(g * wide, wide)], q_sem.at[g]
        )
        copy.start()
        fetch.append(copy)

    barrier = pltpu.get_barrier_semaphore()

    @pl.when(has_far)
    def _():
        pl.semaphore_signal(barrier, inc=1, device_id=behind, device_id_type=MESH)

    @pl.when(has_second)
    def _():
        pl.semaphore_signal(barrier, inc=1, device_id=device(place - 2), device_id_type=MESH)

    pl.semaphore_signal(barrier, inc=1, device_id=partner, device_id_type=MESH)

    doc_copy.wait()
    docs = doc_ref[...].astype(jnp.float32)
    got[OWN, 0, pl.ds(2 * WIDTH, 16)] = jnp.broadcast_to(docs, (16, WIDTH)).astype(jnp.bfloat16)

    for slot, absent in (
        (NEAR, place < 1), (SECOND, place < 2), (FAR, outer < 1), (DISTANT, outer < 2),
    ):

        @pl.when(absent)
        def _(slot=slot):
            got[slot] = jnp.zeros((KV, ROWS, WIDTH), jnp.bfloat16)
            got[slot, 0, pl.ds(2 * WIDTH, 16)] = jnp.full((16, WIDTH), ABSENT, jnp.bfloat16)

    def copy_of(kind, g, source, target):
        rows = pl.ds(0, ROWS if g == 0 else 2 * WIDTH)
        return pltpu.make_async_remote_copy(
            src_ref=got.at[source, g, rows],
            dst_ref=got.at[kind, g, rows],
            send_sem=send_sem.at[kind - 1, g],
            recv_sem=recv_sem.at[kind - 1, g],
            device_id=target,
            device_id_type=MESH,
        )

    def far(g):
        return copy_of(FAR, g, OWN, ahead)

    def distant(g):
        return copy_of(DISTANT, g, FAR, ahead)

    def second(g):
        return copy_of(SECOND, g, OWN, device(place + 2))

    def near(g):
        return copy_of(NEAR, g, OWN, partner)

    def near_back(g):
        return copy_of(NEAR, g, SECOND, partner)

    def on(condition, act):
        @pl.when(condition)
        def _():
            act()

    def send_own(g):
        on(gives_far, lambda: far(g).start())
        on(gives_second, lambda: second(g).start())
        on(core == 0, lambda: near(g).start())

    def pass_on(g):
        on(has_far, lambda: far(g).wait_recv())
        on(has_far & gives_far, lambda: distant(g).start())
        on(has_second, lambda: second(g).wait_recv())
        on((core == 1) & has_second, lambda: near_back(g).start())

    def arrive(g):
        on(has_distant, lambda: distant(g).wait_recv())
        on((core == 1) | has_second, lambda: near(g).wait_recv())

    for copy in staged[:4]:
        copy.wait()

    pl.semaphore_wait(barrier, 1 + gives_far.astype(jnp.int32) + gives_second.astype(jnp.int32))

    send_own(0)
    send_own(1)
    for copy in staged[4:]:
        copy.wait()

    lane = lax.broadcasted_iota(jnp.int32, (WIDTH, WIDTH), 1)
    row = lax.broadcasted_iota(jnp.int32, (WIDTH, WIDTH), 0)
    lane_f = lane.astype(jnp.float32)
    mine = jnp.broadcast_to(docs, (WIDTH, WIDTH))
    mine_down = mine.T
    marks[0] = jnp.where((lane > row) | (mine != mine_down), HIDE, 0.0).astype(jnp.bfloat16)
    marks[1] = jnp.where(lane_f != mine_down, HIDE, 0.0).astype(jnp.bfloat16)
    seen_by[OWN] = jnp.where(lane == row, 1.0, 0.0).astype(jnp.bfloat16)

    def note_documents():
        for slot in (NEAR, SECOND, FAR, DISTANT):
            theirs = got[slot, 0, pl.ds(2 * WIDTH, 16)].astype(jnp.float32)[0:1]
            down = jnp.broadcast_to(theirs, (WIDTH, WIDTH)).T
            seen_by[slot] = jnp.where(lane_f == down, 1.0, 0.0).astype(jnp.bfloat16)

    ones = jnp.ones((WIDTH, WIDTH), jnp.bfloat16)

    def columns(it, i):
        return pl.ds((it * STACK + i) * WIDTH, WIDTH)

    def multiply_keys(it):
        g, slot = it // PER, it % 2
        heads = [queries[:, columns(it, i)] for i in range(STACK)]
        own_side, far_side = (
            jnp.concatenate([jnp.concatenate([q, marks[k]], axis=1) for q in heads], axis=0)
            for k in range(2)
        )

        def key_side(block):
            return jnp.concatenate([got[block, g, pl.ds(0, WIDTH)], seen_by[block]], axis=1)

        scores[slot, :, 0:128] = nt(own_side, key_side(OWN))
        scores[slot, :, 128:384] = nt(
            far_side, jnp.concatenate([key_side(NEAR), key_side(SECOND)], axis=0)
        )
        scores[slot, :, 384:640] = nt(
            far_side, jnp.concatenate([key_side(FAR), key_side(DISTANT)], axis=0)
        )

    def weigh(it):
        slot = it % 2
        for i in range(STACK):
            rows = pl.ds(i * WIDTH, WIDTH)
            s = scores[slot, rows]
            peak = jnp.max(s, axis=1, keepdims=True)
            weights[slot, rows] = jnp.exp2((s - peak) * SCALE2).astype(jnp.bfloat16)
            peaks[...] = jnp.where(lane == it * STACK + i, peak, peaks[...])

    def multiply_values(it):
        g, slot = it // PER, it % 2
        value_side = jnp.concatenate(
            [
                jnp.concatenate([got[block, g, pl.ds(WIDTH, WIDTH)], ones], axis=1)
                for block in range(5)
            ],
            axis=0,
        )
        sums = jnp.dot(weights[slot], value_side, preferred_element_type=jnp.float32)
        for i in range(STACK):
            part = sums[i * WIDTH : (i + 1) * WIDTH]
            total = part[:, WIDTH:]
            result[:, columns(it, i)] = (part[:, :WIDTH] / total).astype(jnp.bfloat16)
            totals[...] = jnp.where(lane == it * STACK + i, total, totals[...])

    def put(g):
        return pltpu.make_async_copy(
            result.at[:, pl.ds(g * wide, wide)], o_hbm.at[:, pl.ds(g * wide, wide)], o_sem.at[g]
        )

    peaks[...] = jnp.zeros_like(peaks)
    totals[...] = jnp.ones_like(totals)
    for it in range(STEPS + 2):
        g = it // PER
        if it < STEPS and it % PER == 0:
            if g == 0:
                pass_on(0)
                send_own(2)
                pass_on(1)
                send_own(3)
            if g + 2 < KV:
                pass
            arrive(g)
            if g == 0:
                note_documents()
            fetch[g].wait()
        if it == PER // 2:
            pass_on(2)
        if it == PER + PER // 2:
            pass_on(3)
        if it >= 2:
            multiply_values(it - 2)
            if (it - 2) % PER == PER - 1:
                put((it - 2) // PER).start()
        if it < STEPS:
            multiply_keys(it)
        if 1 <= it <= STEPS:
            weigh(it - 1)

    log_norm = peaks[...] * SCALE + jnp.log(totals[...])
    log_ref[...] = log_norm.T[0 : KV * GROUP]
    for g in range(KV):
        put(g).wait()
        on(gives_far, lambda: far(g).wait_send())
        on(has_far & gives_far, lambda: distant(g).wait_send())
        on(gives_second, lambda: second(g).wait_send())
        on((core == 0) | has_second, lambda: near(g).wait_send())


def on_device(queries, keys, values, doc_ids):
    block, width = queries.shape
    n_outer, n_inner = lax.axis_size("outer"), lax.axis_size("inner")
    anywhere = pl.BlockSpec(memory_space=pl.ANY)
    vmem = pl.BlockSpec(memory_space=pltpu.VMEM)
    square = (WIDTH, WIDTH)
    return pl.pallas_call(
        functools.partial(kernel, n_outer, n_inner),
        out_shape=(
            jax.ShapeDtypeStruct((block, width), jnp.bfloat16),
            jax.ShapeDtypeStruct((KV * GROUP, block), jnp.float32),
        ),
        in_specs=[anywhere] * 4,
        out_specs=(anywhere, vmem),
        scratch_shapes=[
            pltpu.VMEM((block, width), jnp.bfloat16),
            pltpu.VMEM((block, width), jnp.bfloat16),
            pltpu.VMEM((5, KV, ROWS, WIDTH), jnp.bfloat16),
            pltpu.VMEM((5,) + square, jnp.bfloat16),
            pltpu.VMEM((2,) + square, jnp.bfloat16),
            pltpu.VMEM(square, jnp.float32),
            pltpu.VMEM(square, jnp.float32),
            pltpu.VMEM((2, STACK * WIDTH, 5 * WIDTH), jnp.float32),
            pltpu.VMEM((2, STACK * WIDTH, 5 * WIDTH), jnp.bfloat16),
            pltpu.VMEM((1, WIDTH), jnp.int32),
            pltpu.SemaphoreType.DMA((KV, 2)),
            pltpu.SemaphoreType.DMA((KV,)),
            pltpu.SemaphoreType.DMA((KV,)),
            pltpu.SemaphoreType.DMA,
            pltpu.SemaphoreType.DMA((4, KV)),
            pltpu.SemaphoreType.DMA((4, KV)),
        ],
        compiler_params=pltpu.CompilerParams(
            collective_id=0, has_side_effects=True, vmem_limit_bytes=VMEM
        ),
        name="attention",
    )(queries, keys, values, doc_ids.reshape(1, block))


def solution(mesh):
    split = ("outer", "inner")
    return jax.shard_map(
        on_device,
        mesh=mesh,
        in_specs=(P(split, None), P(split, None), P(split, None), P(split)),
        out_specs=(P(split, None), P(None, split)),
        check_vma=False,
    )
```

```python
import functools
import math

import jax
import jax.numpy as jnp
from jax import lax
from jax.experimental import pallas as pl
from jax.experimental.pallas import tpu as pltpu
from jax.sharding import PartitionSpec as P

MESH = pl.DeviceIdType.MESH
WIDTH = 128
KV = 4
GROUP = 16
STACK = 4
STEPS = KV * GROUP // STACK
PER = GROUP // STACK
HIDE = -65536.0
SCALE = 1.0 / math.sqrt(WIDTH)
SCALE2 = SCALE * math.log2(math.e)
VMEM = 58 * 2**20
ABSENT = 4.0
PLAN = {step: "" for step in range(STEPS + 3)} | {
    0: "L0 F0 S0 N0 L1 F1 S1 N1 L2 L3",
    1: "D0 F2 S2 N2 B0 D1 F3 S3 N3 B1 A0",
    3: "D2 B2",
    5: "A1",
    7: "D3 B3",
    9: "A2",
    13: "A3",
}
ROWS = 2 * WIDTH + 16

OWN, NEAR, SECOND, FAR, DISTANT = range(5)


def nt(a, b):
    return lax.dot_general(a, b, (((1,), (1,)), ((), ())), preferred_element_type=jnp.float32)


def kernel(
    n_outer, n_inner, q_hbm, k_hbm, v_hbm, doc_hbm, result, log_ref,
    queries, got, seen_by, marks, peaks, totals, scores, weights,
    doc_ref, stage_sem, q_sem, doc_sem, send_sem, recv_sem,
):
    outer, inner = lax.axis_index("outer"), lax.axis_index("inner")
    core = lax.rem(inner, 2)
    place = outer * n_inner + inner
    count = n_outer * n_inner

    def device(where):
        where = jnp.clip(where, 0, count - 1)
        return (where // n_inner, lax.rem(where, n_inner))

    has_far, gives_far = outer >= 1, outer < n_outer - 1
    has_distant = outer >= 2
    has_second, gives_second = place >= 2, place + 2 < count
    partner = (outer, inner + 1 - 2 * core)
    ahead = (jnp.minimum(outer + 1, n_outer - 1), inner)
    behind = (jnp.maximum(outer - 1, 0), inner)

    doc_copy = pltpu.make_async_copy(doc_hbm, doc_ref, doc_sem)
    doc_copy.start()
    staged = []
    for g in range(KV):
        for i, ref in enumerate((k_hbm, v_hbm)):
            copy = pltpu.make_async_copy(
                ref.at[:, pl.ds(g * WIDTH, WIDTH)],
                got.at[OWN, g, pl.ds(i * WIDTH, WIDTH)],
                stage_sem.at[g, i],
            )
            copy.start()
            staged.append(copy)
    fetch = []
    wide = GROUP * WIDTH
    for g in range(KV):
        copy = pltpu.make_async_copy(
            q_hbm.at[:, pl.ds(g * wide, wide)], queries.at[:, pl.ds(g * wide, wide)], q_sem.at[g]
        )
        copy.start()
        fetch.append(copy)

    barrier = pltpu.get_barrier_semaphore()

    @pl.when(has_far)
    def _():
        pl.semaphore_signal(barrier, inc=1, device_id=behind, device_id_type=MESH)

    @pl.when(has_second)
    def _():
        pl.semaphore_signal(barrier, inc=1, device_id=device(place - 2), device_id_type=MESH)

    pl.semaphore_signal(barrier, inc=1, device_id=partner, device_id_type=MESH)

    doc_copy.wait()
    docs = doc_ref[...].astype(jnp.float32)
    got[OWN, 0, pl.ds(2 * WIDTH, 16)] = jnp.broadcast_to(docs, (16, WIDTH)).astype(jnp.bfloat16)

    for slot, absent in (
        (NEAR, place < 1), (SECOND, place < 2), (FAR, outer < 1), (DISTANT, outer < 2),
    ):

        @pl.when(absent)
        def _(slot=slot):
            got[slot] = jnp.zeros((KV, ROWS, WIDTH), jnp.bfloat16)
            got[slot, 0, pl.ds(2 * WIDTH, 16)] = jnp.full((16, WIDTH), ABSENT, jnp.bfloat16)

    def copy_of(kind, g, source, target):
        rows = pl.ds(0, ROWS if g == 0 else 2 * WIDTH)
        return pltpu.make_async_remote_copy(
            src_ref=got.at[source, g, rows],
            dst_ref=got.at[kind, g, rows],
            send_sem=send_sem.at[kind - 1, g],
            recv_sem=recv_sem.at[kind - 1, g],
            device_id=target,
            device_id_type=MESH,
        )

    def far(g):
        return copy_of(FAR, g, OWN, ahead)

    def distant(g):
        return copy_of(DISTANT, g, FAR, ahead)

    def second(g):
        return copy_of(SECOND, g, OWN, device(place + 2))

    def near(g):
        return copy_of(NEAR, g, OWN, partner)

    def near_back(g):
        return copy_of(NEAR, g, SECOND, partner)

    def on(condition, act):
        @pl.when(condition)
        def _():
            act()

    def do(word):
        what, g = word[0], int(word[1])
        if what == "L":
            for copy in staged[2 * g : 2 * g + 2]:
                copy.wait()
        elif what == "F":
            on(gives_far, lambda: far(g).start())
        elif what == "S":
            on(gives_second, lambda: second(g).start())
        elif what == "N":
            on(core == 0, lambda: near(g).start())
        elif what == "D":
            on(has_far, lambda: far(g).wait_recv())
            on(has_far & gives_far, lambda: distant(g).start())
        elif what == "B":
            on(has_second, lambda: second(g).wait_recv())
            on((core == 1) & has_second, lambda: near_back(g).start())
        elif what == "A":
            on(has_distant, lambda: distant(g).wait_recv())
            on((core == 1) | has_second, lambda: near(g).wait_recv())
            if g == 0:
                note_documents()
            fetch[g].wait()

    def run_plan(plan):
        for word in plan.split():
            do(word)

    pl.semaphore_wait(barrier, 1 + gives_far.astype(jnp.int32) + gives_second.astype(jnp.int32))

    run_plan(PLAN[0])

    lane = lax.broadcasted_iota(jnp.int32, (WIDTH, WIDTH), 1)
    row = lax.broadcasted_iota(jnp.int32, (WIDTH, WIDTH), 0)
    lane_f = lane.astype(jnp.float32)
    mine = jnp.broadcast_to(docs, (WIDTH, WIDTH))
    mine_down = mine.T
    marks[0] = jnp.where((lane > row) | (mine != mine_down), HIDE, 0.0).astype(jnp.bfloat16)
    marks[1] = jnp.where(lane_f != mine_down, HIDE, 0.0).astype(jnp.bfloat16)
    seen_by[OWN] = jnp.where(lane == row, 1.0, 0.0).astype(jnp.bfloat16)

    def note_documents():
        for slot in (NEAR, SECOND, FAR, DISTANT):
            theirs = got[slot, 0, pl.ds(2 * WIDTH, 16)].astype(jnp.float32)[0:1]
            down = jnp.broadcast_to(theirs, (WIDTH, WIDTH)).T
            seen_by[slot] = jnp.where(lane_f == down, 1.0, 0.0).astype(jnp.bfloat16)

    ones = jnp.ones((WIDTH, WIDTH), jnp.bfloat16)

    def columns(it, i):
        return pl.ds((it * STACK + i) * WIDTH, WIDTH)

    def multiply_keys(it):
        g, slot = it // PER, it % 2
        heads = [queries[:, columns(it, i)] for i in range(STACK)]
        own_side, far_side = (
            jnp.concatenate([jnp.concatenate([q, marks[k]], axis=1) for q in heads], axis=0)
            for k in range(2)
        )

        def key_side(block):
            return jnp.concatenate([got[block, g, pl.ds(0, WIDTH)], seen_by[block]], axis=1)

        scores[slot, :, 0:128] = nt(own_side, key_side(OWN))
        scores[slot, :, 128:384] = nt(
            far_side, jnp.concatenate([key_side(NEAR), key_side(SECOND)], axis=0)
        )
        scores[slot, :, 384:640] = nt(
            far_side, jnp.concatenate([key_side(FAR), key_side(DISTANT)], axis=0)
        )

    def weigh(it):
        slot = it % 2
        for i in range(STACK):
            rows = pl.ds(i * WIDTH, WIDTH)
            s = scores[slot, rows]
            peak = jnp.max(s, axis=1, keepdims=True)
            weights[slot, rows] = jnp.exp2((s - peak) * SCALE2).astype(jnp.bfloat16)
            peaks[...] = jnp.where(lane == it * STACK + i, peak, peaks[...])

    def multiply_values(it):
        g, slot = it // PER, it % 2
        value_side = jnp.concatenate(
            [
                jnp.concatenate([got[block, g, pl.ds(WIDTH, WIDTH)], ones], axis=1)
                for block in range(5)
            ],
            axis=0,
        )
        sums = jnp.dot(weights[slot], value_side, preferred_element_type=jnp.float32)
        for i in range(STACK):
            part = sums[i * WIDTH : (i + 1) * WIDTH]
            total = part[:, WIDTH:]
            result[:, columns(it, i)] = (part[:, :WIDTH] / total).astype(jnp.bfloat16)
            totals[...] = jnp.where(lane == it * STACK + i, total, totals[...])

    peaks[...] = jnp.zeros_like(peaks)
    totals[...] = jnp.ones_like(totals)
    for it in range(STEPS + 2):
        run_plan(PLAN[it + 1])
        if it >= 2:
            multiply_values(it - 2)
        if it < STEPS:
            multiply_keys(it)
        if 1 <= it <= STEPS:
            weigh(it - 1)

    log_norm = peaks[...] * SCALE + jnp.log(totals[...])
    log_ref[...] = log_norm.T[0 : KV * GROUP]
    for g in range(KV):
        on(gives_far, lambda: far(g).wait_send())
        on(has_far & gives_far, lambda: distant(g).wait_send())
        on(gives_second, lambda: second(g).wait_send())
        on((core == 0) | has_second, lambda: near(g).wait_send())


def on_device(queries, keys, values, doc_ids):
    block, width = queries.shape
    n_outer, n_inner = lax.axis_size("outer"), lax.axis_size("inner")
    anywhere = pl.BlockSpec(memory_space=pl.ANY)
    vmem = pl.BlockSpec(memory_space=pltpu.VMEM)
    square = (WIDTH, WIDTH)
    return pl.pallas_call(
        functools.partial(kernel, n_outer, n_inner),
        out_shape=(
            pltpu.VMEM((block, width), jnp.bfloat16),
            pltpu.VMEM((KV * GROUP, block), jnp.float32),
        ),
        in_specs=[anywhere] * 4,
        out_specs=(vmem, vmem),
        scratch_shapes=[
            pltpu.VMEM((block, width), jnp.bfloat16),
            pltpu.VMEM((5, KV, ROWS, WIDTH), jnp.bfloat16),
            pltpu.VMEM((5,) + square, jnp.bfloat16),
            pltpu.VMEM((2,) + square, jnp.bfloat16),
            pltpu.VMEM(square, jnp.float32),
            pltpu.VMEM(square, jnp.float32),
            pltpu.VMEM((2, STACK * WIDTH, 5 * WIDTH), jnp.float32),
            pltpu.VMEM((2, STACK * WIDTH, 5 * WIDTH), jnp.bfloat16),
            pltpu.VMEM((1, WIDTH), jnp.int32),
            pltpu.SemaphoreType.DMA((KV, 2)),
            pltpu.SemaphoreType.DMA((KV,)),
            pltpu.SemaphoreType.DMA,
            pltpu.SemaphoreType.DMA((4, KV)),
            pltpu.SemaphoreType.DMA((4, KV)),
        ],
        compiler_params=pltpu.CompilerParams(
            collective_id=0, has_side_effects=True, vmem_limit_bytes=VMEM
        ),
        name="attention",
    )(queries, keys, values, doc_ids.reshape(1, block))


def solution(mesh):
    split = ("outer", "inner")
    return jax.shard_map(
        on_device,
        mesh=mesh,
        in_specs=(P(split, None), P(split, None), P(split, None), P(split)),
        out_specs=(P(split, None), P(None, split)),
        check_vma=False,
    )
```

```python
import functools
import math

import jax
import jax.numpy as jnp
from jax import lax
from jax.experimental import pallas as pl
from jax.experimental.pallas import tpu as pltpu
from jax.sharding import PartitionSpec as P

MESH = pl.DeviceIdType.MESH
WIDTH = 128
KV = 4
GROUP = 16
STACK = 4
STEPS = KV * GROUP // STACK
PER = GROUP // STACK
HIDE = -65536.0
SCALE = 1.0 / math.sqrt(WIDTH)
SCALE2 = SCALE * math.log2(math.e)
VMEM = 58 * 2**20
ABSENT = 4.0
PLAN = {step: "" for step in range(STEPS + 3)} | {
    0: "L0 L1 L2 L3 T0 T1 T2 T3 E0 E1 E2 E3 F0 S0 N0 F1 S1 N1 S2 N2 S3 N3",
    1: "x0 x1 x2 x3 W0 G0 G1 G2 G3 d0 d1 d2 d3 D0 F2 D1 F3 B0 B1 w0 g0 g1 g2 g3 A0 Q0 Q1",
    3: "D2 B2 Q2",
    5: "A1 Q3",
    7: "D3 B3 R0",
    9: "A2 R1",
    11: "R2",
    13: "A3 R3",
}
ROWS = 2 * WIDTH + 16

OWN, NEAR, SECOND, FAR, DISTANT, PASSING, CROSSING = range(7)
RELAYED = (1, 2, 3)


def nt(a, b):
    return lax.dot_general(a, b, (((1,), (1,)), ((), ())), preferred_element_type=jnp.float32)


def kernel(
    n_outer, n_inner, q_hbm, k_hbm, v_hbm, doc_hbm, result, log_ref,
    queries, got, seen_by, marks, peaks, totals, scores, weights,
    doc_ref, stage_sem, q_sem, doc_sem, send_sem, recv_sem, ready,
):
    outer, inner = lax.axis_index("outer"), lax.axis_index("inner")
    core = lax.rem(inner, 2)
    place = outer * n_inner + inner
    count = n_outer * n_inner

    def device(where):
        where = jnp.clip(where, 0, count - 1)
        return (where // n_inner, lax.rem(where, n_inner))

    has_far, gives_far = outer >= 1, outer < n_outer - 1
    has_distant = outer >= 2
    has_second, gives_second = place >= 2, place + 2 < count
    partner = (outer, inner + 1 - 2 * core)
    half = n_outer // 2
    opens = lax.rem(outer, half) == 0
    follows = lax.rem(outer, half) == 1
    before, middle, relay = outer == half - 1, outer == half, outer == 0
    late = (outer >= half - 1) & (outer <= half + 2)
    hurried = (late & ~middle) | (outer == half - 2)
    ahead = (jnp.minimum(outer + 1, n_outer - 1), inner)
    behind = (jnp.maximum(outer - 1, 0), inner)

    doc_copy = pltpu.make_async_copy(doc_hbm, doc_ref, doc_sem)
    doc_copy.start()
    staged = []
    for g in range(KV):
        for i, ref in enumerate((k_hbm, v_hbm)):
            copy = pltpu.make_async_copy(
                ref.at[:, pl.ds(g * WIDTH, WIDTH)],
                got.at[OWN, g, pl.ds(i * WIDTH, WIDTH)],
                stage_sem.at[g, i],
            )
            copy.start()
            staged.append(copy)
    fetch = []
    wide = GROUP * WIDTH
    for g in range(KV):
        copy = pltpu.make_async_copy(
            q_hbm.at[:, pl.ds(g * wide, wide)], queries.at[:, pl.ds(g * wide, wide)], q_sem.at[g]
        )
        copy.start()
        fetch.append(copy)

    barrier = pltpu.get_barrier_semaphore()

    def greet(condition, target, semaphore=barrier):
        @pl.when(condition)
        def _():
            pl.semaphore_signal(semaphore, inc=1, device_id=target, device_id_type=MESH)

    greet(has_far & ~follows, behind)
    greet(opens, ahead)
    greet(relay, (half - 1, inner))
    greet(middle, (0, inner))
    greet(has_second, device(place - 2))
    greet(place >= 0, partner)

    doc_copy.wait()
    docs = doc_ref[...].astype(jnp.float32)
    got[OWN, 0, pl.ds(2 * WIDTH, 16)] = jnp.broadcast_to(docs, (16, WIDTH)).astype(jnp.bfloat16)

    for slot, absent in (
        (NEAR, place < 1), (SECOND, place < 2), (FAR, outer < 1), (DISTANT, outer < 2),
    ):

        @pl.when(absent)
        def _(slot=slot):
            got[slot] = jnp.zeros((KV, ROWS, WIDTH), jnp.bfloat16)
            got[slot, 0, pl.ds(2 * WIDTH, 16)] = jnp.full((16, WIDTH), ABSENT, jnp.bfloat16)

    def copy_of(kind, g, source, target, landing=None):
        rows = pl.ds(0, ROWS if g == 0 else 2 * WIDTH)
        return pltpu.make_async_remote_copy(
            src_ref=got.at[source, g, rows],
            dst_ref=got.at[landing or kind, g, rows],
            send_sem=send_sem.at[kind - 1, g],
            recv_sem=recv_sem.at[(landing or kind) - 1, g],
            device_id=target,
            device_id_type=MESH,
        )

    def far(g):
        return copy_of(FAR, g, OWN, ahead)

    def distant(g):
        return copy_of(DISTANT, g, FAR, ahead)

    def to_relay(g):
        return copy_of(DISTANT, g, FAR, (0, inner), PASSING)

    def from_relay(g):
        return copy_of(DISTANT, g, PASSING, (half, inner))

    def to_crossing(g):
        return copy_of(FAR, g, OWN, (0, inner), CROSSING)

    def from_crossing(g):
        return copy_of(PASSING, g, CROSSING, (half, inner), FAR)

    def second(g):
        return copy_of(SECOND, g, OWN, device(place + 2))

    def near(g):
        return copy_of(NEAR, g, OWN, partner)

    def near_back(g):
        return copy_of(NEAR, g, SECOND, partner)

    def on(condition, act):
        @pl.when(condition)
        def _():
            act()

    turns = before & (inner >= n_inner - 2)

    def crosses(g):
        return (inner >= 0) if g in RELAYED else (inner < 2)

    def do(word):
        what, g = word[0], int(word[1])
        if what == "L":
            for copy in staged[2 * g : 2 * g + 2]:
                copy.wait()
        elif what == "E":
            on(before & crosses(g), lambda: to_crossing(g).start())
            on(hurried & ~(before & crosses(g)), lambda: far(g).start())
        elif what == "T":
            on(turns, lambda: second(g).start())
        elif what == "F":
            on(gives_far & ~hurried & ~opens, lambda: far(g).start())
        elif what in "Ww":
            on(middle if what == "W" else relay, lambda: pl.semaphore_wait(ready, 1))
        elif what in "Gg":
            on(middle if what == "G" else relay, lambda: far(g).start())
        elif what == "Q":
            on(relay & crosses(g), lambda: to_crossing(g).wait_recv())
            on(relay & crosses(g), lambda: from_crossing(g).start())
        elif what == "R":
            on(relay, lambda: to_relay(g).wait_recv())
            on(relay, lambda: from_relay(g).start())
        elif what == "S":
            on(gives_second & ~turns, lambda: second(g).start())
        elif what == "N":
            on(core == 0, lambda: near(g).start())
        elif what in "Ddx":
            now = {"D": ~late | middle, "d": late & ~before & ~middle, "x": before}[what]
            on(now & has_far, lambda: far(g).wait_recv())
            on(now & has_far & gives_far & ~before, lambda: distant(g).start())
            on(now & before, lambda: to_relay(g).start())
        elif what == "B":
            on(has_second, lambda: second(g).wait_recv())
            on((core == 1) & has_second, lambda: near_back(g).start())
        elif what == "A":
            on(has_distant, lambda: distant(g).wait_recv())
            on((core == 1) | has_second, lambda: near(g).wait_recv())
            if g == 0:
                note_documents()
            fetch[g].wait()

    def run_plan(plan):
        for word in plan.split():
            do(word)

    peers = 1
    for peer in (gives_far & ~opens, follows, before, relay, gives_second):
        peers = peers + peer.astype(jnp.int32)
    pl.semaphore_wait(barrier, peers)
    greet(follows, behind, ready)

    run_plan(PLAN[0])

    lane = lax.broadcasted_iota(jnp.int32, (WIDTH, WIDTH), 1)
    row = lax.broadcasted_iota(jnp.int32, (WIDTH, WIDTH), 0)
    lane_f = lane.astype(jnp.float32)
    mine = jnp.broadcast_to(docs, (WIDTH, WIDTH))
    mine_down = mine.T
    marks[0] = jnp.where((lane > row) | (mine != mine_down), HIDE, 0.0).astype(jnp.bfloat16)
    marks[1] = jnp.where(lane_f != mine_down, HIDE, 0.0).astype(jnp.bfloat16)
    seen_by[OWN] = jnp.where(lane == row, 1.0, 0.0).astype(jnp.bfloat16)

    def note_documents():
        for slot in (NEAR, SECOND, FAR, DISTANT):
            theirs = got[slot, 0, pl.ds(2 * WIDTH, 16)].astype(jnp.float32)[0:1]
            down = jnp.broadcast_to(theirs, (WIDTH, WIDTH)).T
            seen_by[slot] = jnp.where(lane_f == down, 1.0, 0.0).astype(jnp.bfloat16)

    ones = jnp.ones((WIDTH, WIDTH), jnp.bfloat16)

    def columns(it, i):
        return pl.ds((it * STACK + i) * WIDTH, WIDTH)

    def multiply_keys(it):
        g, slot = it // PER, it % 2
        heads = [queries[:, columns(it, i)] for i in range(STACK)]
        own_side, far_side = (
            jnp.concatenate([jnp.concatenate([q, marks[k]], axis=1) for q in heads], axis=0)
            for k in range(2)
        )

        def key_side(block):
            return jnp.concatenate([got[block, g, pl.ds(0, WIDTH)], seen_by[block]], axis=1)

        scores[slot, :, 0:128] = nt(own_side, key_side(OWN))
        scores[slot, :, 128:384] = nt(
            far_side, jnp.concatenate([key_side(NEAR), key_side(SECOND)], axis=0)
        )
        scores[slot, :, 384:640] = nt(
            far_side, jnp.concatenate([key_side(FAR), key_side(DISTANT)], axis=0)
        )

    def weigh(it):
        slot = it % 2
        for i in range(STACK):
            rows = pl.ds(i * WIDTH, WIDTH)
            s = scores[slot, rows]
            peak = jnp.max(s, axis=1, keepdims=True)
            weights[slot, rows] = jnp.exp2((s - peak) * SCALE2).astype(jnp.bfloat16)
            peaks[...] = jnp.where(lane == it * STACK + i, peak, peaks[...])

    def multiply_values(it):
        g, slot = it // PER, it % 2
        value_side = jnp.concatenate(
            [
                jnp.concatenate([got[block, g, pl.ds(WIDTH, WIDTH)], ones], axis=1)
                for block in range(5)
            ],
            axis=0,
        )
        sums = jnp.dot(weights[slot], value_side, preferred_element_type=jnp.float32)
        for i in range(STACK):
            part = sums[i * WIDTH : (i + 1) * WIDTH]
            total = part[:, WIDTH:]
            result[:, columns(it, i)] = (part[:, :WIDTH] / total).astype(jnp.bfloat16)
            totals[...] = jnp.where(lane == it * STACK + i, total, totals[...])

    peaks[...] = jnp.zeros_like(peaks)
    totals[...] = jnp.ones_like(totals)
    for it in range(STEPS + 2):
        run_plan(PLAN[it + 1])
        if it >= 2:
            multiply_values(it - 2)
        if it < STEPS:
            multiply_keys(it)
        if 1 <= it <= STEPS:
            weigh(it - 1)

    log_norm = peaks[...] * SCALE + jnp.log(totals[...])
    log_ref[...] = log_norm.T[0 : KV * GROUP]
    for g in range(KV):
        on(gives_far, lambda: far(g).wait_send())
        on((has_far & gives_far) | relay, lambda: distant(g).wait_send())
        on(relay & crosses(g), lambda: from_crossing(g).wait_send())
        on(gives_second, lambda: second(g).wait_send())
        on((core == 0) | has_second, lambda: near(g).wait_send())


def on_device(queries, keys, values, doc_ids):
    block, width = queries.shape
    n_outer, n_inner = lax.axis_size("outer"), lax.axis_size("inner")
    anywhere = pl.BlockSpec(memory_space=pl.ANY)
    vmem = pl.BlockSpec(memory_space=pltpu.VMEM)
    square = (WIDTH, WIDTH)
    return pl.pallas_call(
        functools.partial(kernel, n_outer, n_inner),
        out_shape=(
            pltpu.VMEM((block, width), jnp.bfloat16),
            pltpu.VMEM((KV * GROUP, block), jnp.float32),
        ),
        in_specs=[anywhere] * 4,
        out_specs=(vmem, vmem),
        scratch_shapes=[
            pltpu.VMEM((block, width), jnp.bfloat16),
            pltpu.VMEM((7, KV, ROWS, WIDTH), jnp.bfloat16),
            pltpu.VMEM((5,) + square, jnp.bfloat16),
            pltpu.VMEM((2,) + square, jnp.bfloat16),
            pltpu.VMEM(square, jnp.float32),
            pltpu.VMEM(square, jnp.float32),
            pltpu.VMEM((2, STACK * WIDTH, 5 * WIDTH), jnp.float32),
            pltpu.VMEM((2, STACK * WIDTH, 5 * WIDTH), jnp.bfloat16),
            pltpu.VMEM((1, WIDTH), jnp.int32),
            pltpu.SemaphoreType.DMA((KV, 2)),
            pltpu.SemaphoreType.DMA((KV,)),
            pltpu.SemaphoreType.DMA,
            pltpu.SemaphoreType.DMA((5, KV)),
            pltpu.SemaphoreType.DMA((6, KV)),
            pltpu.SemaphoreType.REGULAR,
        ],
        compiler_params=pltpu.CompilerParams(
            collective_id=0, has_side_effects=True, vmem_limit_bytes=VMEM
        ),
        name="attention",
    )(queries, keys, values, doc_ids.reshape(1, block))


def solution(mesh):
    split = ("outer", "inner")
    return jax.shard_map(
        on_device,
        mesh=mesh,
        in_specs=(P(split, None), P(split, None), P(split, None), P(split)),
        out_specs=(P(split, None), P(None, split)),
        check_vma=False,
    )
```

```python
import functools
import math

import jax
import jax.numpy as jnp
from jax import lax
from jax.experimental import pallas as pl
from jax.experimental.pallas import tpu as pltpu
from jax.sharding import PartitionSpec as P

MESH = pl.DeviceIdType.MESH
WIDTH = 128
KV = 4
GROUP = 16
STACK = 4
STEPS = KV * GROUP // STACK
PER = GROUP // STACK
HIDE = -65536.0
SCALE = 1.0 / math.sqrt(WIDTH)
SCALE2 = SCALE * math.log2(math.e)
VMEM = 58 * 2**20
ABSENT = 4.0
PLAN = {step: "" for step in range(STEPS + 3)} | {
    0: "L0 L1 L2 L3 T0 T1 T2 T3 E0 E1 E2 E3 F0 S0 N0 F1 S1 N1 S2 N2 S3 N3",
    1: "x0 x1 x2 x3 W0 G0 G1 G2 G3 d0 d1 d2 d3 D0 F2 D1 F3 B0 B1 w0 g0 g1 g2 g3 Q0 Q1 A0",
    3: "D2 B2 Q2",
    5: "A1 Q3",
    7: "D3 B3 R0",
    9: "A2 R1",
    11: "R2",
    13: "A3 R3",
}
ROWS = 2 * WIDTH + 16

OWN, NEAR, SECOND, FAR, DISTANT, PASSING, CROSSING = range(7)
RELAYED = (0, 1, 2, 3)


def nt(a, b):
    return lax.dot_general(a, b, (((1,), (1,)), ((), ())), preferred_element_type=jnp.float32)


def kernel(
    n_outer, n_inner, q_hbm, k_hbm, v_hbm, doc_hbm, result, log_ref,
    queries, got, seen_by, marks, peaks, totals, scores, weights,
    doc_ref, stage_sem, q_sem, doc_sem, send_sem, recv_sem, ready,
):
    outer, inner = lax.axis_index("outer"), lax.axis_index("inner")
    core = lax.rem(inner, 2)
    place = outer * n_inner + inner
    count = n_outer * n_inner

    def device(where):
        where = jnp.clip(where, 0, count - 1)
        return (where // n_inner, lax.rem(where, n_inner))

    has_far, gives_far = outer >= 1, outer < n_outer - 1
    has_distant = outer >= 2
    has_second, gives_second = place >= 2, place + 2 < count
    partner = (outer, inner + 1 - 2 * core)
    half = n_outer // 2
    opens = lax.rem(outer, half) == 0
    follows = lax.rem(outer, half) == 1
    before, middle, relay = outer == half - 1, outer == half, outer == 0
    late = (outer >= half - 1) & (outer <= half + 2)
    hurried = (late & ~middle) | (outer == half - 2)
    ahead = (jnp.minimum(outer + 1, n_outer - 1), inner)
    behind = (jnp.maximum(outer - 1, 0), inner)

    doc_copy = pltpu.make_async_copy(doc_hbm, doc_ref, doc_sem)
    doc_copy.start()
    staged = []
    for g in range(KV):
        for i, ref in enumerate((k_hbm, v_hbm)):
            copy = pltpu.make_async_copy(
                ref.at[:, pl.ds(g * WIDTH, WIDTH)],
                got.at[OWN, g, pl.ds(i * WIDTH, WIDTH)],
                stage_sem.at[g, i],
            )
            copy.start()
            staged.append(copy)
    fetch = []
    wide = GROUP * WIDTH
    for g in range(KV):
        copy = pltpu.make_async_copy(
            q_hbm.at[:, pl.ds(g * wide, wide)], queries.at[:, pl.ds(g * wide, wide)], q_sem.at[g]
        )
        copy.start()
        fetch.append(copy)

    barrier = pltpu.get_barrier_semaphore()

    def greet(condition, target, semaphore=barrier):
        @pl.when(condition)
        def _():
            pl.semaphore_signal(semaphore, inc=1, device_id=target, device_id_type=MESH)

    greet(has_far & ~follows, behind)
    greet(opens, ahead)
    greet(relay, (half - 1, inner))
    greet(middle, (0, inner))
    greet(has_second, device(place - 2))
    greet(place >= 0, partner)

    doc_copy.wait()
    docs = doc_ref[...].astype(jnp.float32)
    got[OWN, 0, pl.ds(2 * WIDTH, 16)] = jnp.broadcast_to(docs, (16, WIDTH)).astype(jnp.bfloat16)

    for slot, absent in (
        (NEAR, place < 1), (SECOND, place < 2), (FAR, outer < 1), (DISTANT, outer < 2),
    ):

        @pl.when(absent)
        def _(slot=slot):
            got[slot] = jnp.zeros((KV, ROWS, WIDTH), jnp.bfloat16)
            got[slot, 0, pl.ds(2 * WIDTH, 16)] = jnp.full((16, WIDTH), ABSENT, jnp.bfloat16)

    def copy_of(kind, g, source, target, landing=None):
        rows = pl.ds(0, ROWS if g == 0 else 2 * WIDTH)
        return pltpu.make_async_remote_copy(
            src_ref=got.at[source, g, rows],
            dst_ref=got.at[landing or kind, g, rows],
            send_sem=send_sem.at[kind - 1, g],
            recv_sem=recv_sem.at[(landing or kind) - 1, g],
            device_id=target,
            device_id_type=MESH,
        )

    def far(g):
        return copy_of(FAR, g, OWN, ahead)

    def distant(g):
        return copy_of(DISTANT, g, FAR, ahead)

    def to_relay(g):
        return copy_of(DISTANT, g, FAR, (0, inner), PASSING)

    def from_relay(g):
        return copy_of(DISTANT, g, PASSING, (half, inner))

    def to_crossing(g):
        return copy_of(FAR, g, OWN, (0, inner), CROSSING)

    def from_crossing(g):
        return copy_of(PASSING, g, CROSSING, (half, inner), FAR)

    def second(g):
        return copy_of(SECOND, g, OWN, device(place + 2))

    def near(g):
        return copy_of(NEAR, g, OWN, partner)

    def near_back(g):
        return copy_of(NEAR, g, SECOND, partner)

    def on(condition, act):
        @pl.when(condition)
        def _():
            act()

    turns = before & (inner >= n_inner - 2)

    def crosses(g):
        return (inner >= 0) if g in RELAYED else (inner < 2)

    def do(word):
        what, g = word[0], int(word[1])
        if what == "L":
            for copy in staged[2 * g : 2 * g + 2]:
                copy.wait()
        elif what == "E":
            on(before & crosses(g), lambda: to_crossing(g).start())
            on(hurried & ~(before & crosses(g)), lambda: far(g).start())
        elif what == "T":
            on(turns, lambda: second(g).start())
        elif what == "F":
            on(gives_far & ~hurried & ~opens, lambda: far(g).start())
        elif what in "Ww":
            on(middle if what == "W" else relay, lambda: pl.semaphore_wait(ready, 1))
        elif what in "Gg":
            on(middle if what == "G" else relay, lambda: far(g).start())
        elif what == "Q":
            on(relay & crosses(g), lambda: to_crossing(g).wait_recv())
            on(relay & crosses(g), lambda: from_crossing(g).start())
        elif what == "R":
            on(relay, lambda: to_relay(g).wait_recv())
            on(relay, lambda: from_relay(g).start())
        elif what == "S":
            on(gives_second & ~turns, lambda: second(g).start())
        elif what == "N":
            on(core == 0, lambda: near(g).start())
        elif what in "Ddx":
            now = {"D": ~late | middle, "d": late & ~before & ~middle, "x": before}[what]
            on(now & has_far, lambda: far(g).wait_recv())
            on(now & has_far & gives_far & ~before, lambda: distant(g).start())
            on(now & before, lambda: to_relay(g).start())
        elif what == "B":
            on(has_second, lambda: second(g).wait_recv())
            on((core == 1) & has_second, lambda: near_back(g).start())
        elif what == "A":
            on(has_distant, lambda: distant(g).wait_recv())
            on((core == 1) | has_second, lambda: near(g).wait_recv())
            if g == 0:
                note_documents()
            fetch[g].wait()

    def run_plan(plan):
        for word in plan.split():
            do(word)

    peers = 1
    for peer in (gives_far & ~opens, follows, before, relay, gives_second):
        peers = peers + peer.astype(jnp.int32)
    pl.semaphore_wait(barrier, peers)
    greet(follows, behind, ready)

    run_plan(PLAN[0])

    lane = lax.broadcasted_iota(jnp.int32, (WIDTH, WIDTH), 1)
    row = lax.broadcasted_iota(jnp.int32, (WIDTH, WIDTH), 0)
    lane_f = lane.astype(jnp.float32)
    mine = jnp.broadcast_to(docs, (WIDTH, WIDTH))
    mine_down = mine.T
    marks[0] = jnp.where((lane > row) | (mine != mine_down), HIDE, 0.0).astype(jnp.bfloat16)
    marks[1] = jnp.where(lane_f != mine_down, HIDE, 0.0).astype(jnp.bfloat16)
    seen_by[OWN] = jnp.where(lane == row, 1.0, 0.0).astype(jnp.bfloat16)

    def note_documents():
        for slot in (NEAR, SECOND, FAR, DISTANT):
            theirs = got[slot, 0, pl.ds(2 * WIDTH, 16)].astype(jnp.float32)[0:1]
            down = jnp.broadcast_to(theirs, (WIDTH, WIDTH)).T
            seen_by[slot] = jnp.where(lane_f == down, 1.0, 0.0).astype(jnp.bfloat16)

    ones = jnp.ones((WIDTH, WIDTH), jnp.bfloat16)

    def columns(it, i):
        return pl.ds((it * STACK + i) * WIDTH, WIDTH)

    def multiply_keys(it):
        g, slot = it // PER, it % 2
        heads = [queries[:, columns(it, i)] for i in range(STACK)]
        own_side, far_side = (
            jnp.concatenate([jnp.concatenate([q, marks[k]], axis=1) for q in heads], axis=0)
            for k in range(2)
        )

        def key_side(block):
            return jnp.concatenate([got[block, g, pl.ds(0, WIDTH)], seen_by[block]], axis=1)

        scores[slot, :, 0:128] = nt(own_side, key_side(OWN))
        scores[slot, :, 128:384] = nt(
            far_side, jnp.concatenate([key_side(NEAR), key_side(SECOND)], axis=0)
        )
        scores[slot, :, 384:640] = nt(
            far_side, jnp.concatenate([key_side(FAR), key_side(DISTANT)], axis=0)
        )

    def weigh(it):
        slot = it % 2
        for i in range(STACK):
            rows = pl.ds(i * WIDTH, WIDTH)
            s = scores[slot, rows]
            peak = jnp.max(s, axis=1, keepdims=True)
            weights[slot, rows] = jnp.exp2((s - peak) * SCALE2).astype(jnp.bfloat16)
            peaks[...] = jnp.where(lane == it * STACK + i, peak, peaks[...])

    def multiply_values(it):
        g, slot = it // PER, it % 2
        value_side = jnp.concatenate(
            [
                jnp.concatenate([got[block, g, pl.ds(WIDTH, WIDTH)], ones], axis=1)
                for block in range(5)
            ],
            axis=0,
        )
        sums = jnp.dot(weights[slot], value_side, preferred_element_type=jnp.float32)
        for i in range(STACK):
            part = sums[i * WIDTH : (i + 1) * WIDTH]
            total = part[:, WIDTH:]
            result[:, columns(it, i)] = (part[:, :WIDTH] / total).astype(jnp.bfloat16)
            totals[...] = jnp.where(lane == it * STACK + i, total, totals[...])

    peaks[...] = jnp.zeros_like(peaks)
    totals[...] = jnp.ones_like(totals)
    for it in range(STEPS + 2):
        run_plan(PLAN[it + 1])
        if it >= 2:
            multiply_values(it - 2)
        if it < STEPS:
            multiply_keys(it)
        if 1 <= it <= STEPS:
            weigh(it - 1)

    log_norm = peaks[...] * SCALE + jnp.log(totals[...])
    log_ref[...] = log_norm.T[0 : KV * GROUP]
    for g in range(KV):
        on(gives_far, lambda: far(g).wait_send())
        on((has_far & gives_far) | relay, lambda: distant(g).wait_send())
        on(relay & crosses(g), lambda: from_crossing(g).wait_send())
        on(gives_second, lambda: second(g).wait_send())
        on((core == 0) | has_second, lambda: near(g).wait_send())


def on_device(queries, keys, values, doc_ids):
    block, width = queries.shape
    n_outer, n_inner = lax.axis_size("outer"), lax.axis_size("inner")
    anywhere = pl.BlockSpec(memory_space=pl.ANY)
    vmem = pl.BlockSpec(memory_space=pltpu.VMEM)
    square = (WIDTH, WIDTH)
    return pl.pallas_call(
        functools.partial(kernel, n_outer, n_inner),
        out_shape=(
            pltpu.VMEM((block, width), jnp.bfloat16),
            pltpu.VMEM((KV * GROUP, block), jnp.float32),
        ),
        in_specs=[anywhere] * 4,
        out_specs=(vmem, vmem),
        scratch_shapes=[
            pltpu.VMEM((block, width), jnp.bfloat16),
            pltpu.VMEM((7, KV, ROWS, WIDTH), jnp.bfloat16),
            pltpu.VMEM((5,) + square, jnp.bfloat16),
            pltpu.VMEM((2,) + square, jnp.bfloat16),
            pltpu.VMEM(square, jnp.float32),
            pltpu.VMEM(square, jnp.float32),
            pltpu.VMEM((2, STACK * WIDTH, 5 * WIDTH), jnp.float32),
            pltpu.VMEM((2, STACK * WIDTH, 5 * WIDTH), jnp.bfloat16),
            pltpu.VMEM((1, WIDTH), jnp.int32),
            pltpu.SemaphoreType.DMA((KV, 2)),
            pltpu.SemaphoreType.DMA((KV,)),
            pltpu.SemaphoreType.DMA,
            pltpu.SemaphoreType.DMA((5, KV)),
            pltpu.SemaphoreType.DMA((6, KV)),
            pltpu.SemaphoreType.REGULAR,
        ],
        compiler_params=pltpu.CompilerParams(
            collective_id=0, has_side_effects=True, vmem_limit_bytes=VMEM
        ),
        name="attention",
    )(queries, keys, values, doc_ids.reshape(1, block))


def solution(mesh):
    split = ("outer", "inner")
    return jax.shard_map(
        on_device,
        mesh=mesh,
        in_specs=(P(split, None), P(split, None), P(split, None), P(split)),
        out_specs=(P(split, None), P(None, split)),
        check_vma=False,
    )
```
